32 devices in a mesh: grp: 2 (over core), dp: 16 (over z, y, x), mp: 1.
Axes of the slice: x: 2, y: 2, z: 4, core: 2. Of those that a mesh axis runs over, the one named last changes fastest.
Arguments:
- states: bfloat16 [2, 32, 128, 4096], P('grp', 'dp'), may hold values from -6 to 6
- loss_grad: bfloat16 [32, 128, 4096], P('dp'), may hold values from -6 to 6
- gains: float32 [2, 4096], P('grp'), may hold values from 0.25 to 1.75
- w_param: bfloat16 [2, 4096, 2048], P('grp', 'dp', 'mp'), may hold values from -0.0234375 to 0.0234375, as said below
- w_fixed: bfloat16 [2, 4096, 2048], P('grp', 'dp', 'mp'), may hold values from -0.09375 to 0.09375
- probes: bfloat16 [2, 4096, 2, 2048], P('grp', 'dp', None, 'mp'), may hold values from -0.0234375 to 0.0234375, as said below
Outputs:
- hv: bfloat16 [2, 4096, 2, 2048], P('grp', 'dp', None, 'mp')
The draws below stay inside these ranges and needn't reach their ends.
Inputs may be any that keep to these rules, and one draw needn't show every extreme that they name: `w_param`: independent entries of mean 0. `probes`: independent entries of mean 0.
All inputs are finite; a program needn't handle non-finite values.
Results may differ from the reference program's by a relative error of at most 0.025.
Values may be sent and summed in bfloat16 or wider, within the bound.
A program may use at most 128 MiB of HBM per device.

```python
import jax
import jax.numpy as jnp
from jax import lax

D = 4096
HEAD = 256
HEADS = 8
PROBES = 2
LEN = 128
SEQ_DEV = 2
SEQS = 32
HD = 2048
N_DP = 16


def folded_entries(key, shape):
    spread = float(D) ** (-0.5) * float(HEAD) ** (-0.25)
    unit = jnp.clip(jax.random.normal(key, shape, jnp.float32), -6.0, 6.0)
    return unit * spread


def draw_w_param(key, part):
    return folded_entries(jax.random.fold_in(key, 11), (2, D, HEADS * HEAD)).astype(jnp.bfloat16)


def draw_probes(key, part):
    return folded_entries(jax.random.fold_in(key, 23), (2, D, PROBES, HEADS * HEAD)).astype(jnp.bfloat16)


def level_of(own_key, shape, shards, least, top_value):
    level = 1.0
    for axis_at, blocks in shards:
        heights = jax.random.uniform(jax.random.fold_in(jax.random.fold_in(own_key, 6), axis_at), (blocks,), jnp.float32, least / len(shards), top_value / len(shards))
        level = level * jnp.repeat(jnp.exp(heights), shape[axis_at] // blocks).reshape((-1,) + (1,) * (len(shape) - 1 - axis_at))
    return level


def centred(stream_key, shape, width, reach, shards=(), kind=jnp.bfloat16):
    entries = width * jax.random.normal(stream_key, shape, jnp.float32)
    if shards:
        entries = entries * level_of(stream_key, shape, shards, -0.22, 0.18)
    return jnp.clip(entries, -reach, reach).astype(kind)


def setup_inputs(seed: int = 0) -> dict:
    key_list = jax.random.split(jax.random.key(seed), 7)
    states = centred(key_list[0], (2, SEQS, LEN, D), 1.0, 6.0, ((0, 2), (1, 16)))
    loss_grad = centred(key_list[1], (SEQS, LEN, D), 1.0, 6.0, ((0, 16),))
    gains = jnp.clip(1.0 + 0.15 * jax.random.normal(key_list[2], (2, D), jnp.float32), 0.25, 1.75)
    w_param = draw_w_param(jax.random.fold_in(key_list[6], 71), 0)
    w_fixed = centred(key_list[4], (2, D, HD), D ** -0.5, 0.09375, ((0, 2), (1, 16)))
    probes = draw_probes(jax.random.fold_in(key_list[6], 71), 0)
    return dict(states=states, loss_grad=loss_grad, gains=gains, w_param=w_param, w_fixed=w_fixed, probes=probes)


EPS = 1e-06

def normalize(rows, gain):
    values = rows.astype(jnp.float32)
    scale = lax.rsqrt(lax.optimization_barrier(jnp.mean(values * values, axis=-1, keepdims=True)) + EPS)
    return (values * scale * gain).astype(jnp.bfloat16)

def attention_loss(query, keys, values, out_grad, scale, weight):
    scores = jnp.einsum('sihe,sjhe->shij', query, keys) * scale
    probs = jax.nn.softmax(scores, axis=-1)
    mixing = jnp.einsum('sihe,sjhe->shij', out_grad, values)
    return jnp.sum(probs * mixing) * weight

def curvature(query, keys, values, out_grad, t_query, t_keys, scale, weight):

    def grads(q_arg, k_arg):
        return jax.grad(attention_loss, argnums=(0, 1))(q_arg, k_arg, values, out_grad, scale, weight)

    def along(a_dir, b_dir):
        return jax.jvp(grads, (query, keys), (a_dir, b_dir))[1]
    return jax.vmap(along)(t_query, t_keys)

def reference(states, loss_grad, gains, w_param, w_fixed, probes):
    rows = SEQS * LEN
    heads_split = (SEQS, LEN, HEADS, HEAD)
    normed = [normalize(states[g].reshape(rows, D), gains[g]) for g in range(2)]
    proj = [jnp.dot(normed[g], w_param[g], preferred_element_type=jnp.float32).astype(jnp.bfloat16) for g in range(2)]
    tang = [jnp.einsum('rd,dpe->rpe', normed[g].astype(jnp.float32), probes[g].astype(jnp.float32)).astype(jnp.bfloat16) for g in range(2)]
    values = jnp.dot(normed[0], w_fixed[0], preferred_element_type=jnp.float32).astype(jnp.bfloat16)
    outgrad = jnp.dot(loss_grad.reshape(rows, D), w_fixed[1], preferred_element_type=jnp.float32).astype(jnp.bfloat16)

    def heads_of(x):
        return x.astype(jnp.float32).reshape(heads_split)

    def probe_heads(x):
        return jnp.moveaxis(x.astype(jnp.float32).reshape(SEQS, LEN, PROBES, HEADS, HEAD), 2, 0)
    scale = 1.0
    weight = float(SEQS * LEN) ** (-0.5)
    d_query, d_keys = curvature(heads_of(proj[1]), heads_of(proj[0]), heads_of(values), heads_of(outgrad), probe_heads(tang[1]), probe_heads(tang[0]), scale, weight)

    def back_rows(x):
        return jnp.moveaxis(x, 0, 2).reshape(rows, PROBES, HD).astype(jnp.bfloat16)
    d_query = back_rows(d_query)
    d_keys = back_rows(d_keys)

    def block_sum(left, right):
        left_blocks = left.reshape(N_DP, SEQ_DEV * LEN, D)
        right_blocks = right.reshape(N_DP, SEQ_DEV * LEN, PROBES, HD)

        def step(total, pair):
            part = jnp.einsum('rd,rpe->dpe', pair[0].astype(jnp.float32), pair[1].astype(jnp.float32))
            part = lax.optimization_barrier(part.astype(jnp.bfloat16)).astype(jnp.float32)
            return (total + part, None)
        total, _ = lax.scan(step, jnp.zeros((D, PROBES, HD), jnp.float32), (left_blocks, right_blocks))
        return total.astype(jnp.bfloat16)
    return jnp.stack([block_sum(normed[0], d_keys), block_sum(normed[1], d_query)])
```

```python
import jax
import jax.numpy as jnp
from jax import lax
from jax.sharding import Mesh, PartitionSpec as P

HEAD = 256


EPS = 1e-06


def normalize(rows, gain):
    values = rows.astype(jnp.float32)
    scale = lax.rsqrt(jnp.mean(values * values, axis=-1, keepdims=True) + EPS)
    return (values * scale * gain).astype(jnp.bfloat16)


def passed_along(value, axis, steps):
    count = lax.axis_size(axis)
    first, last = (max(0, -steps), min(count, count - steps))
    return lax.ppermute(value, axis, [(source, source + steps) for source in range(first, last)])


def attention_loss(query, keys, values, out_grad, weight):
    scores = jnp.einsum("sihe,sjhe->shij", query, keys)
    probs = jax.nn.softmax(scores, axis=-1)
    mixing = jnp.einsum("sihe,sjhe->shij", out_grad, values)
    return jnp.sum(probs * mixing) * weight


def curvature(query, keys, values, out_grad, t_query, t_keys, weight):

    def grads(q_arg, k_arg):
        return jax.grad(attention_loss, argnums=(0, 1))(q_arg, k_arg, values, out_grad, weight)

    def along(a_dir, b_dir):
        return jax.jvp(grads, (query, keys), (a_dir, b_dir))[1]

    return jax.vmap(along)(t_query, t_keys)


def split(dp, heads_here):
    cols = 1
    while cols < 4 and dp % (cols * 2) == 0 and heads_here % (cols * 2) == 0:
        cols *= 2
    return cols, dp // cols


def shards(states, loss_grad, gains, w_param, w_fixed, probes):
    ncol = lax.axis_size("c")
    nrow = lax.axis_size("r")
    is_encoder = lax.axis_index("grp") == 0
    seqs_own, length, width = states.shape[1:]
    rows_own = seqs_own * length
    depth = w_param.shape[1]
    cols_mp = w_param.shape[2]
    cols = cols_mp // ncol
    probe_count = probes.shape[2]
    heads = cols // HEAD
    rows = rows_own * ncol
    seqs = seqs_own * ncol

    normed_own = normalize(states[0].reshape(rows_own, width), gains[0])
    def reorder(x):
        x = x.reshape(rows_own, ncol, nrow, depth)
        return jnp.swapaxes(x, 1, 2).reshape(rows_own, width)

    normed_own = reorder(normed_own)
    source_own = jnp.where(is_encoder, normed_own, reorder(loss_grad))

    wcat = jnp.concatenate([w_param[0][:, None], probes[0], w_fixed[0][:, None]], axis=1)
    wcat = wcat.reshape(depth, 2 + probe_count, ncol, cols)
    wcat = jnp.transpose(wcat, (2, 0, 1, 3)).reshape(ncol, depth, (2 + probe_count) * cols)
    mine = lax.all_to_all(wcat, "c", split_axis=0, concat_axis=0, tiled=True)
    mine = mine.reshape(ncol * depth, (2 + probe_count) * cols)
    w_all = lax.all_gather(mine, "r", axis=0, tiled=True)

    normed = lax.all_gather(normed_own, "c", axis=0, tiled=True)
    source = lax.all_gather(source_own, "c", axis=0, tiled=True)
    wide = (1 + probe_count) * cols
    first = jnp.dot(normed, w_all[:, :wide], preferred_element_type=jnp.float32).astype(jnp.bfloat16)
    second = jnp.dot(source, w_all[:, wide:], preferred_element_type=jnp.float32).astype(jnp.bfloat16)

    k_first, k_second = passed_along((first, second), "grp", 1)

    def heads_of(x):
        return x.astype(jnp.float32).reshape(seqs, length, heads, HEAD)

    def probe_heads(x):
        return jnp.moveaxis(
            x.astype(jnp.float32).reshape(seqs, length, probe_count, heads, HEAD), 2, 0
        )

    def back_rows(x):
        return jnp.moveaxis(x, 0, 2).reshape(rows, probe_count * cols).astype(jnp.bfloat16)

    weight = float(rows_own * ncol * nrow) ** (-0.5)
    d_query, d_keys = curvature(
        heads_of(first[:, :cols]),
        heads_of(k_first[:, :cols]),
        heads_of(k_second),
        heads_of(second),
        probe_heads(first[:, cols:]),
        probe_heads(k_first[:, cols:]),
        weight,
    )
    d_query = back_rows(d_query)
    d_keys = back_rows(d_keys)
    returned = passed_along(d_keys, "grp", -1)
    chosen = jnp.where(is_encoder, returned, d_query)
    part = lax.dot_general(
        normed, chosen, (((0,), (0,)), ((), ())), preferred_element_type=jnp.float32
    ).astype(jnp.bfloat16)
    summed = lax.psum_scatter(part, "r", scatter_dimension=0, tiled=True)
    summed = summed.reshape(ncol, depth, probe_count * cols)
    out = lax.all_to_all(summed, "c", split_axis=0, concat_axis=0, tiled=True)
    out = jnp.transpose(out.reshape(ncol, depth, probe_count, cols), (1, 2, 0, 3))
    return out.reshape(1, depth, probe_count, cols_mp)


def solution(mesh):
    grp, dp, mp = (mesh.shape[name] for name in ("grp", "dp", "mp"))

    def run(states, loss_grad, gains, w_param, w_fixed, probes):
        ncol, nrow = split(dp, w_param.shape[2] // mp // HEAD)
        fine = Mesh(mesh.devices.reshape(grp, ncol, nrow, mp), ("grp", "c", "r", "mp"))
        in_specs = (
            P("grp", ("c", "r"), None, None),
            P(("c", "r"), None, None),
            P("grp", None),
            P("grp", ("c", "r"), "mp"),
            P("grp", ("c", "r"), "mp"),
            P("grp", ("c", "r"), None, "mp"),
        )
        out_specs = P("grp", ("c", "r"), None, "mp")
        return jax.shard_map(shards, mesh=fine, in_specs=in_specs, out_specs=out_specs, check_vma=False)(
            states, loss_grad, gains, w_param, w_fixed, probes
        )

    return run
```

```python
import functools

import jax
import jax.numpy as jnp
from jax import lax
from jax.experimental import pallas as pl
from jax.experimental.pallas import tpu as pltpu
from jax.sharding import PartitionSpec as P

HEAD = 256


EPS = 1e-06
MESH = pl.DeviceIdType.MESH


def normalize(rows, gain):
    values = rows.astype(jnp.float32)
    scale = lax.rsqrt(jnp.mean(values * values, axis=-1, keepdims=True) + EPS)
    return (values * scale * gain).astype(jnp.bfloat16)


def passed_along(value, axis, steps):
    count = lax.axis_size(axis)
    first, last = (max(0, -steps), min(count, count - steps))
    return lax.ppermute(value, axis, [(source, source + steps) for source in range(first, last)])


def attention_loss(query, keys, values, out_grad, weight):
    scores = jnp.einsum("sihe,sjhe->shij", query, keys)
    probs = jax.nn.softmax(scores, axis=-1)
    mixing = jnp.einsum("sihe,sjhe->shij", out_grad, values)
    return jnp.sum(probs * mixing) * weight


def curvature(query, keys, values, out_grad, t_query, t_keys, weight):

    def grads(q_arg, k_arg):
        return jax.grad(attention_loss, argnums=(0, 1))(q_arg, k_arg, values, out_grad, weight)

    def along(a_dir, b_dir):
        return jax.jvp(grads, (query, keys), (a_dir, b_dir))[1]

    return jax.vmap(along)(t_query, t_keys)


class Split:
    def __init__(self, dp, heads_here):
        bits = dp.bit_length() - 1
        assert dp == 1 << bits
        col = []
        for bit in range(0, bits, 2):
            if len(col) < 2 and heads_here % (2 << len(col)) == 0:
                col.append(1 << bit)
        self.col = col[::-1]
        self.row = [1 << bit for bit in reversed(range(bits)) if 1 << bit not in col]
        self.ncol = 1 << len(col)
        self.nrow = 1 << len(self.row)

    def col_mask(self, offset):
        return [b for i, b in enumerate(self.col) if (offset >> i) & 1]

    def row_mask(self, offset):
        return [b for i, b in enumerate(self.row) if (offset >> i) & 1]

    def col_index(self, index):
        return sum((((index // b) % 2) * (1 << i) for i, b in enumerate(self.col)), 0)


def flipped(index, masks):
    for b in masks:
        index = index + b - 2 * b * ((index // b) % 2)
    return index


def greet(me, split):
    peers = [split.col_mask(o) for o in range(1, split.ncol)] + [[b] for b in split.row]
    barrier = pltpu.get_barrier_semaphore()
    for masks in peers:
        pl.semaphore_signal(
            barrier, inc=1, device_id={"dp": flipped(me, masks)}, device_id_type=MESH
        )
    pl.semaphore_wait(barrier, len(peers))


def gather_kernel(split, pieces, w_ref, n_ref, g_ref, w_out, n_out, g_out,
                  w_send, w_recv, n_send, n_recv, g_send, g_recv, own_sem):
    me = lax.axis_index("dp")
    decoder = lax.axis_index("grp") != 0
    depth = w_ref.shape[1]
    ncol, nrow = split.ncol, split.nrow
    my_col = split.col_index(me)
    rows = n_ref.shape[0]
    piece = rows // pieces

    def weight_slot(cs, ro):
        source = flipped(flipped(me, split.col_mask(cs)), split.row_mask(ro))
        return w_out.at[pl.ds(pl.multiple_of(source * depth, depth), depth)]

    def row_slot(out, co, k):
        source = split.col_index(flipped(me, split.col_mask(co)))
        return out.at[pl.ds(pl.multiple_of(source * rows + k * piece, piece), piece)]

    def remote(src, dst, send, recv, masks):
        return pltpu.make_async_remote_copy(
            src_ref=src, dst_ref=dst, send_sem=send, recv_sem=recv,
            device_id={"dp": flipped(me, masks)}, device_id_type=MESH,
        )

    greet(me, split)

    sent = []
    gsent = []

    def weight_copy(cs, ro):
        if ro == 0:
            dest = split.col_index(flipped(me, split.col_mask(cs)))
            return remote(w_ref.at[dest], weight_slot(0, 0), w_send.at[cs, 0], w_recv.at[cs, 0],
                          split.col_mask(cs))
        stage = ro.bit_length() - 1
        held = ro - (1 << stage)
        src = w_ref.at[my_col] if (cs, held) == (0, 0) else weight_slot(cs, held)
        return remote(src, weight_slot(cs, held), w_send.at[cs, ro], w_recv.at[cs, ro],
                      [split.row[stage]])

    def row_copy(own, out, send, recv, co, k):
        stage = co.bit_length() - 1
        held = co - (1 << stage)
        src = own.at[pl.ds(k * piece, piece)] if held == 0 else row_slot(out, held, k)
        return remote(src, row_slot(out, held, k), send.at[co, k], recv.at[co, k],
                      [split.col[stage]])

    def start_weight(cs, ro):
        copy = weight_copy(cs, ro)
        copy.start()
        sent.append(copy)

    def start_row(co, k):
        copy = row_copy(n_ref, n_out, n_send, n_recv, co, k)
        copy.start()
        sent.append(copy)
        gcopy = row_copy(g_ref, g_out, g_send, g_recv, co, k)

        @pl.when(decoder)
        def _():
            gcopy.start()

        gsent.append(gcopy)

    row_stages = len(split.row)
    col_stages = len(split.col)

    def have_weight(cs, ro):
        first = ro.bit_length()
        for stage in range(first, row_stages):
            start_weight(cs, ro + (1 << stage))

    def have_row(co, k):
        for stage in range(co.bit_length(), col_stages):
            start_row(co + (1 << stage), k)

    for cs in range(1, ncol):
        start_weight(cs, 0)
    have_weight(0, 0)
    for k in range(pieces):
        have_row(0, k)

    own = [
        pltpu.make_async_copy(w_ref.at[my_col], weight_slot(0, 0), own_sem.at[0]),
        pltpu.make_async_copy(
            n_ref, n_out.at[pl.ds(pl.multiple_of(my_col * rows, rows), rows)], own_sem.at[1]
        ),
        pltpu.make_async_copy(
            g_ref, g_out.at[pl.ds(pl.multiple_of(my_col * rows, rows), rows)], own_sem.at[2]
        ),
    ]
    for copy in own:
        copy.start()

    weights = sorted(
        ((cs, ro) for cs in range(ncol) for ro in range(nrow) if (cs, ro) != (0, 0)),
        key=lambda b: (b[1].bit_length() + (1 if b[0] else 0), b[1], b[0]),
    )
    row_steps = sorted(
        ((co, k) for co in range(1, ncol) for k in range(pieces)),
        key=lambda b: (b[0].bit_length(), b[1], b[0]),
    )
    order = sorted(
        [((i + 1) / len(weights), 0, b) for i, b in enumerate(weights)]
        + [((i + 1) / max(1, len(row_steps)), 1, b) for i, b in enumerate(row_steps)]
    )
    for _, kind, block in order:
        if kind == 0:
            weight_copy(*block).wait_recv()
            have_weight(*block)
        else:
            row_copy(n_ref, n_out, n_send, n_recv, *block).wait_recv()
            gcopy = row_copy(g_ref, g_out, g_send, g_recv, *block)

            @pl.when(decoder)
            def _():
                gcopy.wait_recv()

            have_row(*block)

    for copy in own:
        copy.wait()
    for copy in sent:
        copy.wait_send()
    for copy in gsent:
        @pl.when(decoder)
        def _():
            copy.wait_send()


def gather(split, weights, normed, grads):
    ncol, depth, wide = weights.shape
    rows, width = normed.shape
    pieces = 2
    hbm = pl.BlockSpec(memory_space=pl.ANY)
    dma = pltpu.SemaphoreType.DMA
    return pl.pallas_call(
        functools.partial(gather_kernel, split, pieces),
        out_shape=(
            jax.ShapeDtypeStruct((width, wide), weights.dtype),
            jax.ShapeDtypeStruct((ncol * rows, width), normed.dtype),
            jax.ShapeDtypeStruct((ncol * rows, width), grads.dtype),
        ),
        in_specs=[hbm] * 3,
        out_specs=(hbm,) * 3,
        scratch_shapes=[
            dma((ncol, split.nrow)), dma((ncol, split.nrow)),
            dma((ncol, pieces)), dma((ncol, pieces)),
            dma((ncol, pieces)), dma((ncol, pieces)),
            dma((3,)),
        ],
        compiler_params=pltpu.CompilerParams(collective_id=0, has_side_effects=True),
        name="gather",
    )(weights, normed, grads)


def scatter_kernel(split, p_ref, o_ref, land, held, send, recv, out_send, out_recv, own_sem):
    me = lax.axis_index("dp")
    ncol = split.ncol
    depth = o_ref.shape[1]
    stages = list(reversed(range(len(split.row))))
    my_col = split.col_index(me)
    strip = 64

    def slot(co, ro):
        block = flipped(flipped(me, split.col_mask(co)), split.row_mask(ro))
        return pl.multiple_of(block * depth, depth)

    def copy_of(co, ro):
        stage = ro.bit_length() - 1
        kept = ro - (1 << stage)
        first = stage == stages[0]
        src = p_ref.at[pl.ds(slot(co, ro), depth)] if first else held.at[co, ro]
        return pltpu.make_async_remote_copy(
            src_ref=src, dst_ref=land.at[co, ro], send_sem=send.at[co, ro], recv_sem=recv.at[co, ro],
            device_id={"dp": flipped(me, [split.row[stage]])}, device_id_type=MESH,
        )

    def out_copy(co):
        src = held.at[co, 0]
        return pltpu.make_async_remote_copy(
            src_ref=src, dst_ref=o_ref.at[my_col], send_sem=out_send.at[co], recv_sem=out_recv.at[co],
            device_id={"dp": flipped(me, split.col_mask(co))}, device_id_type=MESH,
        )

    greet(me, split)
    copies = []
    top = 1 << stages[0]
    order = list(reversed(range(ncol)))
    for ro in reversed(range(top)):
        for co in order:
            copy = copy_of(co, top + ro)
            copy.start()
            copies.append(copy)
    for stage in stages:
        bit = 1 << stage
        for ro in reversed(range(bit)):
            for co in order:
                copy_of(co, bit + ro).wait_recv()
                base = slot(co, ro)
                first = stage == stages[0]

                @pl.loop(0, depth // strip)
                def _(i):
                    at = pl.ds(pl.multiple_of(i * strip, strip), strip)
                    if first:
                        mine = p_ref[pl.ds(pl.multiple_of(base + i * strip, strip), strip)]
                    else:
                        mine = held[co, ro, at]
                    other = land[co, bit + ro, at]
                    held[co, ro, at] = (
                        mine.astype(jnp.float32) + other.astype(jnp.float32)
                    ).astype(jnp.bfloat16)

                if ro and ro.bit_length() == stage:
                    copy = copy_of(co, ro)
                    copy.start()
                    copies.append(copy)
                elif ro == 0 and stage == 0:
                    if co:
                        copy = out_copy(co)
                        copy.start()
                        copies.append(copy)
                    else:
                        own = pltpu.make_async_copy(held.at[0, 0], o_ref.at[my_col], own_sem)
                        own.start()
    for co in range(1, ncol):
        out_copy(co).wait_recv()
    own.wait()
    for copy in copies:
        copy.wait_send()


def scatter(split, part, depth):
    ncol, nrow = split.ncol, split.nrow
    wide = part.shape[1]
    dma = pltpu.SemaphoreType.DMA
    vmem = pl.BlockSpec(memory_space=pltpu.VMEM)
    return pl.pallas_call(
        functools.partial(scatter_kernel, split),
        out_shape=jax.ShapeDtypeStruct((ncol, depth, wide), part.dtype),
        in_specs=[vmem],
        out_specs=vmem,
        scratch_shapes=[
            pltpu.VMEM((ncol, nrow, depth, wide), part.dtype),
            pltpu.VMEM((ncol, nrow // 2, depth, wide), part.dtype),
            dma((ncol, nrow)), dma((ncol, nrow)), dma((ncol,)), dma((ncol,)), dma,
        ],
        compiler_params=pltpu.CompilerParams(
            collective_id=1, has_side_effects=True, vmem_limit_bytes=48 * 1024 * 1024
        ),
        name="scatter",
    )(part)


def shards(split, states, loss_grad, gains, w_param, w_fixed, probes):
    ncol, nrow = split.ncol, split.nrow
    is_encoder = lax.axis_index("grp") == 0
    seqs_own, length, width = states.shape[1:]
    rows_own = seqs_own * length
    depth = w_param.shape[1]
    cols_mp = w_param.shape[2]
    cols = cols_mp // ncol
    probe_count = probes.shape[2]
    heads = cols // HEAD
    rows = rows_own * ncol
    seqs = seqs_own * ncol

    normed_own = normalize(states[0].reshape(rows_own, width), gains[0])
    grads_own = loss_grad.reshape(rows_own, width)

    wcat = jnp.concatenate([w_param[0][:, None], probes[0], w_fixed[0][:, None]], axis=1)
    wcat = wcat.reshape(depth, 2 + probe_count, ncol, cols)
    wcat = jnp.transpose(wcat, (2, 0, 1, 3)).reshape(ncol, depth, (2 + probe_count) * cols)
    w_all, normed, grads = gather(split, wcat, normed_own, grads_own)
    source = jnp.where(is_encoder, normed, grads)

    wide = (1 + probe_count) * cols
    first = jnp.dot(normed, w_all[:, :wide], preferred_element_type=jnp.float32).astype(jnp.bfloat16)
    second = jnp.dot(source, w_all[:, wide:], preferred_element_type=jnp.float32).astype(jnp.bfloat16)

    k_first, k_second = passed_along((first, second), "grp", 1)

    def heads_of(x):
        return x.astype(jnp.float32).reshape(seqs, length, heads, HEAD)

    def probe_heads(x):
        return jnp.moveaxis(
            x.astype(jnp.float32).reshape(seqs, length, probe_count, heads, HEAD), 2, 0
        )

    def back_rows(x):
        return jnp.moveaxis(x, 0, 2).reshape(rows, probe_count * cols).astype(jnp.bfloat16)

    weight = float(rows_own * ncol * nrow) ** (-0.5)
    d_query, d_keys = curvature(
        heads_of(first[:, :cols]),
        heads_of(k_first[:, :cols]),
        heads_of(k_second),
        heads_of(second),
        probe_heads(first[:, cols:]),
        probe_heads(k_first[:, cols:]),
        weight,
    )
    d_query = back_rows(d_query)
    d_keys = back_rows(d_keys)
    returned = passed_along(d_keys, "grp", -1)
    chosen = jnp.where(is_encoder, returned, d_query)
    part = lax.dot_general(
        normed, chosen, (((0,), (0,)), ((), ())), preferred_element_type=jnp.float32
    ).astype(jnp.bfloat16)
    out = scatter(split, part, depth)
    out = jnp.transpose(out.reshape(ncol, depth, probe_count, cols), (1, 2, 0, 3))
    return out.reshape(1, depth, probe_count, cols_mp)


def solution(mesh):
    dp, mp = (mesh.shape[name] for name in ("dp", "mp"))
    in_specs = (
        P("grp", "dp", None, None),
        P("dp", None, None),
        P("grp", None),
        P("grp", "dp", "mp"),
        P("grp", "dp", "mp"),
        P("grp", "dp", None, "mp"),
    )
    out_specs = P("grp", "dp", None, "mp")

    def run(states, loss_grad, gains, w_param, w_fixed, probes):
        split = Split(dp, w_param.shape[2] // mp // HEAD)
        return jax.shard_map(
            functools.partial(shards, split),
            mesh=mesh, in_specs=in_specs, out_specs=out_specs, check_vma=False,
        )(states, loss_grad, gains, w_param, w_fixed, probes)

    return run
```

```python
import functools

import jax
import jax.numpy as jnp
from jax import lax
from jax.experimental import pallas as pl
from jax.experimental.pallas import tpu as pltpu
from jax.sharding import PartitionSpec as P

HEAD = 256


EPS = 1e-06
MESH = pl.DeviceIdType.MESH


def normalize(rows, gain):
    values = rows.astype(jnp.float32)
    scale = lax.rsqrt(jnp.mean(values * values, axis=-1, keepdims=True) + EPS)
    return (values * scale * gain).astype(jnp.bfloat16)


def swapped(value):
    return lax.ppermute(value, "grp", [(0, 1), (1, 0)])


def attention_kernel(heads, probe_count, weight, keep, keep_last, other, other_last, own, theirs):
    encoder = lax.axis_index("grp") == 0
    cols = heads * HEAD

    def dot(a, b, dims):
        return lax.dot_general(a, b, ((dims[0], dims[1]), ((), ())), preferred_element_type=jnp.float32)

    nt, nn, tn = ((1,), (1,)), ((1,), (0,)), ((0,), (0,))

    def sides(mine, yours, at):
        x, y = mine[:, at : at + HEAD], yours[:, at : at + HEAD]
        return jnp.where(encoder, x, y), jnp.where(encoder, y, x)

    for h in range(heads):
        at = h * HEAD
        k, q = sides(keep, other, at)
        v, o = sides(keep_last, other_last, at)
        scores = dot(q, k, nt)
        top = jnp.exp(scores - jnp.max(scores, axis=-1, keepdims=True))
        probs = top / jnp.sum(top, axis=-1, keepdims=True)
        mixing = dot(o, v, nt)
        centred = mixing - jnp.sum(probs * mixing, axis=-1, keepdims=True)
        grad = (probs * centred * weight).astype(jnp.bfloat16)
        for p in range(probe_count):
            pat = (1 + p) * cols + at
            tk, tq = sides(keep, other, pat)
            d_scores = dot(tq, k, nt) + dot(q, tk, nt)
            d_probs = probs * (d_scores - jnp.sum(probs * d_scores, axis=-1, keepdims=True))
            d_mean = jnp.sum(d_probs * mixing, axis=-1, keepdims=True)
            d_grad = ((d_probs * centred - probs * d_mean) * weight).astype(jnp.bfloat16)
            dq = (dot(d_grad, k, nn) + dot(grad, tk, nn)).astype(jnp.bfloat16)
            dk = (dot(d_grad, q, tn) + dot(grad, tq, tn)).astype(jnp.bfloat16)
            out = p * cols + at
            own[:, out : out + HEAD] = jnp.where(encoder, dk, dq)
            theirs[:, out : out + HEAD] = jnp.where(encoder, dq, dk)


def attention(keep, keep_last, other, other_last, length, probe_count, weight):
    rows, cols = keep_last.shape
    heads = cols // HEAD

    def block(width):
        return pl.BlockSpec((length, width), lambda s: (s, 0))

    wide, out = keep.shape[1], probe_count * cols
    shape = jax.ShapeDtypeStruct((rows, out), jnp.bfloat16)
    return pl.pallas_call(
        functools.partial(attention_kernel, heads, probe_count, weight),
        grid=(rows // length,),
        out_shape=(shape, shape),
        in_specs=[block(wide), block(cols), block(wide), block(cols)],
        out_specs=(block(out), block(out)),
        compiler_params=pltpu.CompilerParams(vmem_limit_bytes=32 * 1024 * 1024),
        name="attention",
    )(keep, keep_last, other, other_last)


class Split:
    def __init__(self, dp, heads_here):
        bits = dp.bit_length() - 1
        assert dp == 1 << bits
        col = []
        for bit in range(0, bits, 2):
            if len(col) < 2 and heads_here % (2 << len(col)) == 0:
                col.append(1 << bit)
        self.col = col[::-1]
        self.row = [1 << bit for bit in reversed(range(bits)) if 1 << bit not in col]
        self.ncol = 1 << len(col)
        self.nrow = 1 << len(self.row)

    def col_mask(self, offset):
        return [b for i, b in enumerate(self.col) if (offset >> i) & 1]

    def row_mask(self, offset):
        return [b for i, b in enumerate(self.row) if (offset >> i) & 1]

    def col_index(self, index):
        return sum((((index // b) % 2) * (1 << i) for i, b in enumerate(self.col)), 0)


def flipped(index, masks):
    for b in masks:
        index = index + b - 2 * b * ((index // b) % 2)
    return index


def greet(me, split):
    peers = [split.col_mask(o) for o in range(1, split.ncol)] + [[b] for b in split.row]
    barrier = pltpu.get_barrier_semaphore()
    for masks in peers:
        pl.semaphore_signal(
            barrier, inc=1, device_id={"dp": flipped(me, masks)}, device_id_type=MESH
        )
    pl.semaphore_wait(barrier, len(peers))


def gather_kernel(split, pieces, w_ref, n_ref, g_ref, w_out, n_out, g_out,
                  w_send, w_recv, n_send, n_recv, g_send, g_recv, own_sem):
    me = lax.axis_index("dp")
    decoder = lax.axis_index("grp") != 0
    ncol, nrow = split.ncol, split.nrow
    depth = w_ref.shape[0]
    wide = w_ref.shape[1] // ncol
    my_col = split.col_index(me)
    rows = n_ref.shape[0]
    piece = rows // pieces

    def weight_own(col):
        return w_ref.at[:, pl.ds(pl.multiple_of(col * wide, wide), wide)]

    def weight_slot(cs, ro):
        source = flipped(flipped(me, split.col_mask(cs)), split.row_mask(ro))
        return w_out.at[pl.ds(pl.multiple_of(source * depth, depth), depth)]

    def row_slot(out, co, k):
        source = split.col_index(flipped(me, split.col_mask(co)))
        return out.at[pl.ds(pl.multiple_of(source * rows + k * piece, piece), piece)]

    def remote(src, dst, send, recv, masks):
        return pltpu.make_async_remote_copy(
            src_ref=src, dst_ref=dst, send_sem=send, recv_sem=recv,
            device_id={"dp": flipped(me, masks)}, device_id_type=MESH,
        )

    greet(me, split)

    sent = []
    gsent = []

    def weight_copy(cs, ro):
        if ro == 0:
            dest = split.col_index(flipped(me, split.col_mask(cs)))
            return remote(weight_own(dest), weight_slot(0, 0), w_send.at[cs, 0], w_recv.at[cs, 0],
                          split.col_mask(cs))
        stage = ro.bit_length() - 1
        held = ro - (1 << stage)
        src = weight_own(my_col) if (cs, held) == (0, 0) else weight_slot(cs, held)
        return remote(src, weight_slot(cs, held), w_send.at[cs, ro], w_recv.at[cs, ro],
                      [split.row[stage]])

    def row_copy(own, out, send, recv, co, k):
        stage = co.bit_length() - 1
        held = co - (1 << stage)
        src = own.at[pl.ds(k * piece, piece)] if held == 0 else row_slot(out, held, k)
        return remote(src, row_slot(out, held, k), send.at[co, k], recv.at[co, k],
                      [split.col[stage]])

    def start_weight(cs, ro):
        copy = weight_copy(cs, ro)
        copy.start()
        sent.append(copy)

    def start_row(co, k):
        copy = row_copy(n_ref, n_out, n_send, n_recv, co, k)
        copy.start()
        sent.append(copy)
        gcopy = row_copy(g_ref, g_out, g_send, g_recv, co, k)

        @pl.when(decoder)
        def _():
            gcopy.start()

        gsent.append(gcopy)

    row_stages = len(split.row)
    col_stages = len(split.col)

    def have_weight(cs, ro):
        first = ro.bit_length()
        for stage in range(first, row_stages):
            start_weight(cs, ro + (1 << stage))

    def have_row(co, k):
        for stage in range(co.bit_length(), col_stages):
            start_row(co + (1 << stage), k)

    for cs in range(1, ncol):
        start_weight(cs, 0)
    have_weight(0, 0)
    for k in range(pieces):
        have_row(0, k)

    own = [
        pltpu.make_async_copy(weight_own(my_col), weight_slot(0, 0), own_sem.at[0]),
        pltpu.make_async_copy(
            n_ref, n_out.at[pl.ds(pl.multiple_of(my_col * rows, rows), rows)], own_sem.at[1]
        ),
        pltpu.make_async_copy(
            g_ref, g_out.at[pl.ds(pl.multiple_of(my_col * rows, rows), rows)], own_sem.at[2]
        ),
    ]
    for copy in own:
        copy.start()

    weights = sorted(
        ((cs, ro) for cs in range(ncol) for ro in range(nrow) if (cs, ro) != (0, 0)),
        key=lambda b: (b[1].bit_length() + (1 if b[0] else 0), b[1], b[0]),
    )
    row_steps = sorted(
        ((co, k) for co in range(1, ncol) for k in range(pieces)),
        key=lambda b: (b[0].bit_length(), b[1], b[0]),
    )
    order = sorted(
        [((i + 1) / len(weights), 0, b) for i, b in enumerate(weights)]
        + [((i + 1) / max(1, len(row_steps)), 1, b) for i, b in enumerate(row_steps)]
    )
    for _, kind, block in order:
        if kind == 0:
            weight_copy(*block).wait_recv()
            have_weight(*block)
        else:
            row_copy(n_ref, n_out, n_send, n_recv, *block).wait_recv()
            gcopy = row_copy(g_ref, g_out, g_send, g_recv, *block)

            @pl.when(decoder)
            def _():
                gcopy.wait_recv()

            have_row(*block)

    for copy in own:
        copy.wait()
    for copy in sent:
        copy.wait_send()
    for copy in gsent:
        @pl.when(decoder)
        def _():
            copy.wait_send()


def gather(split, weights, normed, grads):
    ncol, wide = split.ncol, weights.shape[1] // split.ncol
    rows, width = normed.shape
    pieces = 2
    hbm = pl.BlockSpec(memory_space=pl.ANY)
    dma = pltpu.SemaphoreType.DMA
    return pl.pallas_call(
        functools.partial(gather_kernel, split, pieces),
        out_shape=(
            jax.ShapeDtypeStruct((width, wide), weights.dtype),
            jax.ShapeDtypeStruct((ncol * rows, width), normed.dtype),
            jax.ShapeDtypeStruct((ncol * rows, width), grads.dtype),
        ),
        in_specs=[hbm] * 3,
        out_specs=(hbm,) * 3,
        scratch_shapes=[
            dma((ncol, split.nrow)), dma((ncol, split.nrow)),
            dma((ncol, pieces)), dma((ncol, pieces)),
            dma((ncol, pieces)), dma((ncol, pieces)),
            dma((3,)),
        ],
        compiler_params=pltpu.CompilerParams(collective_id=0, has_side_effects=True),
        name="gather",
    )(weights, normed, grads)


def scatter_kernel(split, p_ref, o_ref, land, held, send, recv, out_send, out_recv, own_sem):
    me = lax.axis_index("dp")
    ncol = split.ncol
    depth = o_ref.shape[1]
    stages = list(reversed(range(len(split.row))))
    my_col = split.col_index(me)
    strip = 64

    def slot(co, ro):
        block = flipped(flipped(me, split.col_mask(co)), split.row_mask(ro))
        return pl.multiple_of(block * depth, depth)

    def copy_of(co, ro):
        stage = ro.bit_length() - 1
        kept = ro - (1 << stage)
        first = stage == stages[0]
        src = p_ref.at[pl.ds(slot(co, ro), depth)] if first else held.at[co, ro]
        return pltpu.make_async_remote_copy(
            src_ref=src, dst_ref=land.at[co, ro], send_sem=send.at[co, ro], recv_sem=recv.at[co, ro],
            device_id={"dp": flipped(me, [split.row[stage]])}, device_id_type=MESH,
        )

    def out_copy(co):
        src = held.at[co, 0]
        return pltpu.make_async_remote_copy(
            src_ref=src, dst_ref=o_ref.at[my_col], send_sem=out_send.at[co], recv_sem=out_recv.at[co],
            device_id={"dp": flipped(me, split.col_mask(co))}, device_id_type=MESH,
        )

    greet(me, split)
    copies = []
    top = 1 << stages[0]
    order = list(reversed(range(ncol)))
    for ro in reversed(range(top)):
        for co in order:
            copy = copy_of(co, top + ro)
            copy.start()
            copies.append(copy)
    for stage in stages:
        bit = 1 << stage
        for ro in reversed(range(bit)):
            for co in order:
                copy_of(co, bit + ro).wait_recv()
                base = slot(co, ro)
                first = stage == stages[0]

                @pl.loop(0, depth // strip)
                def _(i):
                    at = pl.ds(pl.multiple_of(i * strip, strip), strip)
                    if first:
                        mine = p_ref[pl.ds(pl.multiple_of(base + i * strip, strip), strip)]
                    else:
                        mine = held[co, ro, at]
                    other = land[co, bit + ro, at]
                    held[co, ro, at] = (
                        mine.astype(jnp.float32) + other.astype(jnp.float32)
                    ).astype(jnp.bfloat16)

                if ro and ro.bit_length() == stage:
                    copy = copy_of(co, ro)
                    copy.start()
                    copies.append(copy)
                elif ro == 0 and stage == 0:
                    if co:
                        copy = out_copy(co)
                        copy.start()
                        copies.append(copy)
                    else:
                        own = pltpu.make_async_copy(held.at[0, 0], o_ref.at[my_col], own_sem)
                        own.start()
    for co in range(1, ncol):
        out_copy(co).wait_recv()
    own.wait()
    for copy in copies:
        copy.wait_send()


def scatter(split, part, depth):
    ncol, nrow = split.ncol, split.nrow
    wide = part.shape[1]
    dma = pltpu.SemaphoreType.DMA
    vmem = pl.BlockSpec(memory_space=pltpu.VMEM)
    return pl.pallas_call(
        functools.partial(scatter_kernel, split),
        out_shape=jax.ShapeDtypeStruct((ncol, depth, wide), part.dtype),
        in_specs=[vmem],
        out_specs=vmem,
        scratch_shapes=[
            pltpu.VMEM((ncol, nrow, depth, wide), part.dtype),
            pltpu.VMEM((ncol, nrow // 2, depth, wide), part.dtype),
            dma((ncol, nrow)), dma((ncol, nrow)), dma((ncol,)), dma((ncol,)), dma,
        ],
        compiler_params=pltpu.CompilerParams(
            collective_id=1, has_side_effects=True, vmem_limit_bytes=48 * 1024 * 1024
        ),
        name="scatter",
    )(part)


def shards(split, states, loss_grad, gains, w_param, w_fixed, probes):
    ncol, nrow = split.ncol, split.nrow
    is_encoder = lax.axis_index("grp") == 0
    seqs_own, length, width = states.shape[1:]
    rows_own = seqs_own * length
    depth = w_param.shape[1]
    cols_mp = w_param.shape[2]
    cols = cols_mp // ncol
    probe_count = probes.shape[2]
    rows = rows_own * ncol

    normed_own = normalize(states[0].reshape(rows_own, width), gains[0])
    grads_own = loss_grad.reshape(rows_own, width)

    units = [w_param[0], *(probes[0, :, p] for p in range(probe_count)), w_fixed[0]]
    wcat = jnp.concatenate(
        [unit[:, c * cols : (c + 1) * cols] for c in range(ncol) for unit in units], axis=1
    )
    w_all, normed, grads = gather(split, wcat, normed_own, grads_own)
    source = jnp.where(is_encoder, normed, grads)

    wide = (1 + probe_count) * cols
    first = jnp.dot(normed, w_all[:, :wide], preferred_element_type=jnp.float32).astype(jnp.bfloat16)
    second = jnp.dot(source, w_all[:, wide:], preferred_element_type=jnp.float32).astype(jnp.bfloat16)

    half = rows // 2
    grp = lax.axis_index("grp")

    def halves(x):
        keep = lax.dynamic_slice_in_dim(x, grp * half, half, 0)
        return keep, swapped(lax.dynamic_slice_in_dim(x, (1 - grp) * half, half, 0))

    keep, other = halves(first)
    keep_last, other_last = halves(second)
    weight = float(rows_own * ncol * nrow) ** (-0.5)
    own, theirs = attention(keep, keep_last, other, other_last, length, probe_count, weight)
    back = swapped(theirs)
    chosen = jnp.concatenate(
        [jnp.where(is_encoder, own, back), jnp.where(is_encoder, back, own)], axis=0
    )
    part = lax.dot_general(
        normed, chosen, (((0,), (0,)), ((), ())), preferred_element_type=jnp.float32
    ).astype(jnp.bfloat16)
    out = scatter(split, part, depth)
    out = jnp.transpose(out.reshape(ncol, depth, probe_count, cols), (1, 2, 0, 3))
    return out.reshape(1, depth, probe_count, cols_mp)


def solution(mesh):
    dp, mp = (mesh.shape[name] for name in ("dp", "mp"))
    in_specs = (
        P("grp", "dp", None, None),
        P("dp", None, None),
        P("grp", None),
        P("grp", "dp", "mp"),
        P("grp", "dp", "mp"),
        P("grp", "dp", None, "mp"),
    )
    out_specs = P("grp", "dp", None, "mp")

    def run(states, loss_grad, gains, w_param, w_fixed, probes):
        split = Split(dp, w_param.shape[2] // mp // HEAD)
        return jax.shard_map(
            functools.partial(shards, split),
            mesh=mesh, in_specs=in_specs, out_specs=out_specs, check_vma=False,
        )(states, loss_grad, gains, w_param, w_fixed, probes)

    return run
```

```python
import functools

import jax
import jax.numpy as jnp
from jax import lax
from jax.experimental import pallas as pl
from jax.experimental.pallas import tpu as pltpu
from jax.sharding import PartitionSpec as P

HEAD = 256


EPS = 1e-06
MESH = pl.DeviceIdType.MESH


def normalize(rows, gain):
    values = rows.astype(jnp.float32)
    scale = lax.rsqrt(jnp.mean(values * values, axis=-1, keepdims=True) + EPS)
    return (values * scale * gain).astype(jnp.bfloat16)


def swapped(value):
    return lax.ppermute(value, "grp", [(0, 1), (1, 0)])


def attention_kernel(heads, probe_count, weight, keep, keep_last, other, other_last, own, theirs):
    encoder = lax.axis_index("grp") == 0
    cols = heads * HEAD

    def dot(a, b, dims):
        return lax.dot_general(a, b, ((dims[0], dims[1]), ((), ())), preferred_element_type=jnp.float32)

    nt, nn, tn = ((1,), (1,)), ((1,), (0,)), ((0,), (0,))

    def sides(mine, yours, at):
        x, y = mine[:, at : at + HEAD], yours[:, at : at + HEAD]
        return jnp.where(encoder, x, y), jnp.where(encoder, y, x)

    for h in range(heads):
        at = h * HEAD
        k, q = sides(keep, other, at)
        v, o = sides(keep_last, other_last, at)
        scores = dot(q, k, nt)
        top = jnp.exp(scores - jnp.max(scores, axis=-1, keepdims=True))
        probs = top / jnp.sum(top, axis=-1, keepdims=True)
        mixing = dot(o, v, nt)
        centred = mixing - jnp.sum(probs * mixing, axis=-1, keepdims=True)
        grad = (probs * centred * weight).astype(jnp.bfloat16)
        for p in range(probe_count):
            pat = (1 + p) * cols + at
            tk, tq = sides(keep, other, pat)
            d_scores = dot(tq, k, nt) + dot(q, tk, nt)
            d_probs = probs * (d_scores - jnp.sum(probs * d_scores, axis=-1, keepdims=True))
            d_mean = jnp.sum(d_probs * mixing, axis=-1, keepdims=True)
            d_grad = ((d_probs * centred - probs * d_mean) * weight).astype(jnp.bfloat16)
            dq = (dot(d_grad, k, nn) + dot(grad, tk, nn)).astype(jnp.bfloat16)
            dk = (dot(d_grad, q, tn) + dot(grad, tq, tn)).astype(jnp.bfloat16)
            out = p * cols + at
            own[:, out : out + HEAD] = jnp.where(encoder, dk, dq)
            theirs[:, out : out + HEAD] = jnp.where(encoder, dq, dk)


def attention(keep, keep_last, other, other_last, length, probe_count, weight):
    rows, cols = keep_last.shape
    heads = cols // HEAD

    def block(width):
        return pl.BlockSpec((length, width), lambda s: (s, 0))

    wide, out = keep.shape[1], probe_count * cols
    shape = jax.ShapeDtypeStruct((rows, out), jnp.bfloat16)
    return pl.pallas_call(
        functools.partial(attention_kernel, heads, probe_count, weight),
        grid=(rows // length,),
        out_shape=(shape, shape),
        in_specs=[block(wide), block(cols), block(wide), block(cols)],
        out_specs=(block(out), block(out)),
        compiler_params=pltpu.CompilerParams(vmem_limit_bytes=32 * 1024 * 1024),
        name="attention",
    )(keep, keep_last, other, other_last)


class Split:
    def __init__(self, dp, heads_here):
        bits = dp.bit_length() - 1
        assert dp == 1 << bits
        col = []
        for bit in range(0, bits, 2):
            if len(col) < 2 and heads_here % (2 << len(col)) == 0:
                col.append(1 << bit)
        self.col = col[::-1]
        self.row = [1 << bit for bit in reversed(range(bits)) if 1 << bit not in col]
        self.ncol = 1 << len(col)
        self.nrow = 1 << len(self.row)

    def col_mask(self, offset):
        return [b for i, b in enumerate(self.col) if (offset >> i) & 1]

    def row_mask(self, offset):
        return [b for i, b in enumerate(self.row) if (offset >> i) & 1]

    def col_index(self, index):
        return sum((((index // b) % 2) * (1 << i) for i, b in enumerate(self.col)), 0)


def flipped(index, masks):
    for b in masks:
        index = index + b - 2 * b * ((index // b) % 2)
    return index


def greet(me, split):
    peers = [split.col_mask(o) for o in range(1, split.ncol)] + [[b] for b in split.row]
    barrier = pltpu.get_barrier_semaphore()
    for masks in peers:
        pl.semaphore_signal(
            barrier, inc=1, device_id={"dp": flipped(me, masks)}, device_id_type=MESH
        )
    pl.semaphore_wait(barrier, len(peers))


def gather_kernel(split, pieces, w_ref, n_ref, g_ref, w_out, n_out, g_out,
                  w_send, w_recv, n_send, n_recv, g_send, g_recv, own_sem):
    me = lax.axis_index("dp")
    decoder = lax.axis_index("grp") != 0
    ncol, nrow = split.ncol, split.nrow
    depth = w_ref.shape[0]
    wide = w_ref.shape[1] // ncol
    my_col = split.col_index(me)
    rows = n_ref.shape[0]
    piece = rows // pieces

    def weight_own(col):
        return w_ref.at[:, pl.ds(pl.multiple_of(col * wide, wide), wide)]

    def weight_slot(cs, ro):
        source = flipped(flipped(me, split.col_mask(cs)), split.row_mask(ro))
        return w_out.at[pl.ds(pl.multiple_of(source * depth, depth), depth)]

    def row_slot(out, co, k):
        source = split.col_index(flipped(me, split.col_mask(co)))
        return out.at[pl.ds(pl.multiple_of(source * rows + k * piece, piece), piece)]

    def remote(src, dst, send, recv, masks):
        return pltpu.make_async_remote_copy(
            src_ref=src, dst_ref=dst, send_sem=send, recv_sem=recv,
            device_id={"dp": flipped(me, masks)}, device_id_type=MESH,
        )

    greet(me, split)

    sent = []
    gsent = []

    def weight_copy(cs, ro):
        if ro == 0:
            dest = split.col_index(flipped(me, split.col_mask(cs)))
            return remote(weight_own(dest), weight_slot(0, 0), w_send.at[cs, 0], w_recv.at[cs, 0],
                          split.col_mask(cs))
        stage = ro.bit_length() - 1
        held = ro - (1 << stage)
        src = weight_own(my_col) if (cs, held) == (0, 0) else weight_slot(cs, held)
        return remote(src, weight_slot(cs, held), w_send.at[cs, ro], w_recv.at[cs, ro],
                      [split.row[stage]])

    def row_copy(own, out, send, recv, co, k):
        stage = co.bit_length() - 1
        held = co - (1 << stage)
        src = own.at[pl.ds(k * piece, piece)] if held == 0 else row_slot(out, held, k)
        return remote(src, row_slot(out, held, k), send.at[co, k], recv.at[co, k],
                      [split.col[stage]])

    def start_weight(cs, ro):
        copy = weight_copy(cs, ro)
        copy.start()
        sent.append(copy)

    def start_row(co, k):
        copy = row_copy(n_ref, n_out, n_send, n_recv, co, k)
        copy.start()
        sent.append(copy)
        gcopy = row_copy(g_ref, g_out, g_send, g_recv, co, k)

        @pl.when(decoder)
        def _():
            gcopy.start()

        gsent.append(gcopy)

    row_stages = len(split.row)
    col_stages = len(split.col)

    def have_weight(cs, ro):
        first = ro.bit_length()
        for stage in range(first, row_stages):
            start_weight(cs, ro + (1 << stage))

    def have_row(co, k):
        for stage in range(co.bit_length(), col_stages):
            start_row(co + (1 << stage), k)

    for cs in range(1, ncol):
        start_weight(cs, 0)
    have_weight(0, 0)

    own = [
        pltpu.make_async_copy(weight_own(my_col), weight_slot(0, 0), own_sem.at[0]),
        pltpu.make_async_copy(
            n_ref, n_out.at[pl.ds(pl.multiple_of(my_col * rows, rows), rows)], own_sem.at[1]
        ),
        pltpu.make_async_copy(
            g_ref, g_out.at[pl.ds(pl.multiple_of(my_col * rows, rows), rows)], own_sem.at[2]
        ),
    ]
    for copy in own:
        copy.start()

    for cs in range(1, ncol):
        weight_copy(cs, 0).wait_recv()
        have_weight(cs, 0)
        for stage in range(col_stages):
            if cs == 1 << stage:
                for k in range(pieces):
                    start_row(cs, k)

    weights = [(ro.bit_length() == row_stages, ro, cs) for ro in range(1, nrow) for cs in range(ncol)]
    row_steps = [(co.bit_length() == col_stages, co, k) for co in range(1, ncol) for k in range(pieces)]
    order = []
    for last in (False, True):
        some = sorted(w for w in weights if w[0] == last)
        order += [(last, (i + 1) / len(some), 0, (cs, ro)) for i, (_, ro, cs) in enumerate(some)]
        some = sorted(r for r in row_steps if r[0] == last)
        order += [(last, (i + 1) / len(some), 1, (co, k)) for i, (_, co, k) in enumerate(some)]
    order = [entry[1:] for entry in sorted(order)]
    for _, kind, block in order:
        if kind == 0:
            weight_copy(*block).wait_recv()
            have_weight(*block)
        else:
            row_copy(n_ref, n_out, n_send, n_recv, *block).wait_recv()
            gcopy = row_copy(g_ref, g_out, g_send, g_recv, *block)

            @pl.when(decoder)
            def _():
                gcopy.wait_recv()

            have_row(*block)

    for copy in own:
        copy.wait()
    for copy in sent:
        copy.wait_send()
    for copy in gsent:
        @pl.when(decoder)
        def _():
            copy.wait_send()


def gather(split, weights, normed, grads):
    ncol, wide = split.ncol, weights.shape[1] // split.ncol
    rows, width = normed.shape
    pieces = 2
    hbm = pl.BlockSpec(memory_space=pl.ANY)
    dma = pltpu.SemaphoreType.DMA
    return pl.pallas_call(
        functools.partial(gather_kernel, split, pieces),
        out_shape=(
            jax.ShapeDtypeStruct((width, wide), weights.dtype),
            jax.ShapeDtypeStruct((ncol * rows, width), normed.dtype),
            jax.ShapeDtypeStruct((ncol * rows, width), grads.dtype),
        ),
        in_specs=[hbm] * 3,
        out_specs=(hbm,) * 3,
        scratch_shapes=[
            dma((ncol, split.nrow)), dma((ncol, split.nrow)),
            dma((ncol, pieces)), dma((ncol, pieces)),
            dma((ncol, pieces)), dma((ncol, pieces)),
            dma((3,)),
        ],
        compiler_params=pltpu.CompilerParams(collective_id=0, has_side_effects=True),
        name="gather",
    )(weights, normed, grads)


def scatter_kernel(split, p_ref, o_ref, land, held, send, recv, out_send, out_recv, own_sem):
    me = lax.axis_index("dp")
    ncol = split.ncol
    depth = o_ref.shape[1]
    stages = list(reversed(range(len(split.row))))
    my_col = split.col_index(me)
    strip = 64

    def slot(co, ro):
        block = flipped(flipped(me, split.col_mask(co)), split.row_mask(ro))
        return pl.multiple_of(block * depth, depth)

    def copy_of(co, ro):
        stage = ro.bit_length() - 1
        kept = ro - (1 << stage)
        first = stage == stages[0]
        src = p_ref.at[pl.ds(slot(co, ro), depth)] if first else held.at[co, ro]
        return pltpu.make_async_remote_copy(
            src_ref=src, dst_ref=land.at[co, ro], send_sem=send.at[co, ro], recv_sem=recv.at[co, ro],
            device_id={"dp": flipped(me, [split.row[stage]])}, device_id_type=MESH,
        )

    def out_copy(co):
        src = held.at[co, 0]
        return pltpu.make_async_remote_copy(
            src_ref=src, dst_ref=o_ref.at[my_col], send_sem=out_send.at[co], recv_sem=out_recv.at[co],
            device_id={"dp": flipped(me, split.col_mask(co))}, device_id_type=MESH,
        )

    greet(me, split)
    copies = []
    top = 1 << stages[0]
    order = list(reversed(range(ncol)))
    for ro in reversed(range(top)):
        for co in order:
            copy = copy_of(co, top + ro)
            copy.start()
            copies.append(copy)
    for stage in stages:
        bit = 1 << stage
        for ro in reversed(range(bit)):
            for co in order:
                copy_of(co, bit + ro).wait_recv()
                base = slot(co, ro)
                first = stage == stages[0]

                @pl.loop(0, depth // strip)
                def _(i):
                    at = pl.ds(pl.multiple_of(i * strip, strip), strip)
                    if first:
                        mine = p_ref[pl.ds(pl.multiple_of(base + i * strip, strip), strip)]
                    else:
                        mine = held[co, ro, at]
                    other = land[co, bit + ro, at]
                    held[co, ro, at] = (
                        mine.astype(jnp.float32) + other.astype(jnp.float32)
                    ).astype(jnp.bfloat16)

                if ro and ro.bit_length() == stage:
                    copy = copy_of(co, ro)
                    copy.start()
                    copies.append(copy)
                elif ro == 0 and stage == 0:
                    if co:
                        copy = out_copy(co)
                        copy.start()
                        copies.append(copy)
                    else:
                        own = pltpu.make_async_copy(held.at[0, 0], o_ref.at[my_col], own_sem)
                        own.start()
    for co in range(1, ncol):
        out_copy(co).wait_recv()
    own.wait()
    for copy in copies:
        copy.wait_send()


def scatter(split, part, depth):
    ncol, nrow = split.ncol, split.nrow
    wide = part.shape[1]
    dma = pltpu.SemaphoreType.DMA
    vmem = pl.BlockSpec(memory_space=pltpu.VMEM)
    return pl.pallas_call(
        functools.partial(scatter_kernel, split),
        out_shape=jax.ShapeDtypeStruct((ncol, depth, wide), part.dtype),
        in_specs=[vmem],
        out_specs=vmem,
        scratch_shapes=[
            pltpu.VMEM((ncol, nrow, depth, wide), part.dtype),
            pltpu.VMEM((ncol, nrow // 2, depth, wide), part.dtype),
            dma((ncol, nrow)), dma((ncol, nrow)), dma((ncol,)), dma((ncol,)), dma,
        ],
        compiler_params=pltpu.CompilerParams(
            collective_id=1, has_side_effects=True, vmem_limit_bytes=48 * 1024 * 1024
        ),
        name="scatter",
    )(part)


def shards(split, states, loss_grad, gains, w_param, w_fixed, probes):
    ncol, nrow = split.ncol, split.nrow
    is_encoder = lax.axis_index("grp") == 0
    seqs_own, length, width = states.shape[1:]
    rows_own = seqs_own * length
    depth = w_param.shape[1]
    cols_mp = w_param.shape[2]
    cols = cols_mp // ncol
    probe_count = probes.shape[2]
    rows = rows_own * ncol

    normed_own = normalize(states[0].reshape(rows_own, width), gains[0])
    grads_own = loss_grad.reshape(rows_own, width)

    units = [w_param[0], *(probes[0, :, p] for p in range(probe_count)), w_fixed[0]]
    wcat = jnp.concatenate(
        [unit[:, c * cols : (c + 1) * cols] for c in range(ncol) for unit in units], axis=1
    )
    w_all, normed, grads = gather(split, wcat, normed_own, grads_own)
    source = jnp.where(is_encoder, normed, grads)

    wide = (1 + probe_count) * cols
    first = jnp.dot(normed, w_all[:, :wide], preferred_element_type=jnp.float32).astype(jnp.bfloat16)
    second = jnp.dot(source, w_all[:, wide:], preferred_element_type=jnp.float32).astype(jnp.bfloat16)

    half = rows // 2
    grp = lax.axis_index("grp")

    def halves(x):
        keep = lax.dynamic_slice_in_dim(x, grp * half, half, 0)
        return keep, swapped(lax.dynamic_slice_in_dim(x, (1 - grp) * half, half, 0))

    keep, other = halves(first)
    keep_last, other_last = halves(second)
    weight = float(rows_own * ncol * nrow) ** (-0.5)
    own, theirs = attention(keep, keep_last, other, other_last, length, probe_count, weight)
    back = swapped(theirs)
    chosen = jnp.concatenate(
        [jnp.where(is_encoder, own, back), jnp.where(is_encoder, back, own)], axis=0
    )
    part = lax.dot_general(
        normed, chosen, (((0,), (0,)), ((), ())), preferred_element_type=jnp.float32
    ).astype(jnp.bfloat16)
    out = scatter(split, part, depth)
    out = jnp.transpose(out.reshape(ncol, depth, probe_count, cols), (1, 2, 0, 3))
    return out.reshape(1, depth, probe_count, cols_mp)


def solution(mesh):
    dp, mp = (mesh.shape[name] for name in ("dp", "mp"))
    in_specs = (
        P("grp", "dp", None, None),
        P("dp", None, None),
        P("grp", None),
        P("grp", "dp", "mp"),
        P("grp", "dp", "mp"),
        P("grp", "dp", None, "mp"),
    )
    out_specs = P("grp", "dp", None, "mp")

    def run(states, loss_grad, gains, w_param, w_fixed, probes):
        split = Split(dp, w_param.shape[2] // mp // HEAD)
        return jax.shard_map(
            functools.partial(shards, split),
            mesh=mesh, in_specs=in_specs, out_specs=out_specs, check_vma=False,
        )(states, loss_grad, gains, w_param, w_fixed, probes)

    return run
```

```python
import functools

import jax
import jax.numpy as jnp
from jax import lax
from jax.experimental import pallas as pl
from jax.experimental.pallas import tpu as pltpu
from jax.sharding import PartitionSpec as P

HEAD = 256


EPS = 1e-06
MESH = pl.DeviceIdType.MESH


def normalize(rows, gain):
    values = rows.astype(jnp.float32)
    scale = lax.rsqrt(jnp.mean(values * values, axis=-1, keepdims=True) + EPS)
    return (values * scale * gain).astype(jnp.bfloat16)


def swapped(value):
    return lax.ppermute(value, "grp", [(0, 1), (1, 0)])


def attention_kernel(heads, probe_count, weight, keep, keep_last, other, other_last, own, theirs):
    encoder = lax.axis_index("grp") == 0
    cols = heads * HEAD

    def dot(a, b, dims):
        return lax.dot_general(a, b, ((dims[0], dims[1]), ((), ())), preferred_element_type=jnp.float32)

    nt, nn, tn = ((1,), (1,)), ((1,), (0,)), ((0,), (0,))

    def sides(mine, yours, at):
        x, y = mine[:, at : at + HEAD], yours[:, at : at + HEAD]
        return jnp.where(encoder, x, y), jnp.where(encoder, y, x)

    for h in range(heads):
        at = h * HEAD
        k, q = sides(keep, other, at)
        v, o = sides(keep_last, other_last, at)
        scores = dot(q, k, nt)
        top = jnp.exp(scores - jnp.max(scores, axis=-1, keepdims=True))
        probs = top / jnp.sum(top, axis=-1, keepdims=True)
        mixing = dot(o, v, nt)
        centred = mixing - jnp.sum(probs * mixing, axis=-1, keepdims=True)
        grad = (probs * centred * weight).astype(jnp.bfloat16)
        for p in range(probe_count):
            pat = (1 + p) * cols + at
            tk, tq = sides(keep, other, pat)
            d_scores = dot(tq, k, nt) + dot(q, tk, nt)
            d_probs = probs * (d_scores - jnp.sum(probs * d_scores, axis=-1, keepdims=True))
            d_mean = jnp.sum(d_probs * mixing, axis=-1, keepdims=True)
            d_grad = ((d_probs * centred - probs * d_mean) * weight).astype(jnp.bfloat16)
            dq = (dot(d_grad, k, nn) + dot(grad, tk, nn)).astype(jnp.bfloat16)
            dk = (dot(d_grad, q, tn) + dot(grad, tq, tn)).astype(jnp.bfloat16)
            out = p * cols + at
            own[:, out : out + HEAD] = jnp.where(encoder, dk, dq)
            theirs[:, out : out + HEAD] = jnp.where(encoder, dq, dk)


def attention(keep, keep_last, other, other_last, length, probe_count, weight):
    rows, cols = keep_last.shape
    heads = cols // HEAD

    def block(width):
        return pl.BlockSpec((length, width), lambda s: (s, 0))

    wide, out = keep.shape[1], probe_count * cols
    shape = jax.ShapeDtypeStruct((rows, out), jnp.bfloat16)
    return pl.pallas_call(
        functools.partial(attention_kernel, heads, probe_count, weight),
        grid=(rows // length,),
        out_shape=(shape, shape),
        in_specs=[block(wide), block(cols), block(wide), block(cols)],
        out_specs=(block(out), block(out)),
        compiler_params=pltpu.CompilerParams(vmem_limit_bytes=32 * 1024 * 1024),
        name="attention",
    )(keep, keep_last, other, other_last)


class Split:
    def __init__(self, dp, heads_here):
        bits = dp.bit_length() - 1
        assert dp == 1 << bits
        col = []
        for bit in range(0, bits, 2):
            if len(col) < 2 and heads_here % (2 << len(col)) == 0:
                col.append(1 << bit)
        self.col = col[::-1]
        self.row = [1 << bit for bit in reversed(range(bits)) if 1 << bit not in col]
        self.ncol = 1 << len(col)
        self.nrow = 1 << len(self.row)

    def col_mask(self, offset):
        return [b for i, b in enumerate(self.col) if (offset >> i) & 1]

    def row_mask(self, offset):
        return [b for i, b in enumerate(self.row) if (offset >> i) & 1]

    def col_index(self, index):
        return sum((((index // b) % 2) * (1 << i) for i, b in enumerate(self.col)), 0)


def flipped(index, masks):
    for b in masks:
        index = index + b - 2 * b * ((index // b) % 2)
    return index


def greet(me, split):
    peers = [split.col_mask(o) for o in range(1, split.ncol)] + [[b] for b in split.row]
    barrier = pltpu.get_barrier_semaphore()
    for masks in peers:
        pl.semaphore_signal(
            barrier, inc=1, device_id={"dp": flipped(me, masks)}, device_id_type=MESH
        )
    pl.semaphore_wait(barrier, len(peers))


def gather_kernel(split, pieces, w_ref, n_ref, g_ref, w_out, n_out, g_out,
                  w_send, w_recv, n_send, n_recv, g_send, g_recv, own_sem):
    me = lax.axis_index("dp")
    decoder = lax.axis_index("grp") != 0
    ncol, nrow = split.ncol, split.nrow
    depth = w_ref.shape[0]
    wide = w_ref.shape[1] // ncol
    my_col = split.col_index(me)
    rows = n_ref.shape[0]
    piece = rows // pieces

    def weight_own(col):
        return w_ref.at[:, pl.ds(pl.multiple_of(col * wide, wide), wide)]

    def weight_slot(cs, ro):
        source = flipped(flipped(me, split.col_mask(cs)), split.row_mask(ro))
        return w_out.at[pl.ds(pl.multiple_of(source * depth, depth), depth)]

    def row_slot(out, co, k):
        source = split.col_index(flipped(me, split.col_mask(co)))
        return out.at[pl.ds(pl.multiple_of(source * rows + k * piece, piece), piece)]

    def remote(src, dst, send, recv, masks):
        return pltpu.make_async_remote_copy(
            src_ref=src, dst_ref=dst, send_sem=send, recv_sem=recv,
            device_id={"dp": flipped(me, masks)}, device_id_type=MESH,
        )

    greet(me, split)

    sent = []
    gsent = []

    def weight_copy(cs, ro):
        if ro == 0:
            dest = split.col_index(flipped(me, split.col_mask(cs)))
            return remote(weight_own(dest), weight_slot(0, 0), w_send.at[cs, 0], w_recv.at[cs, 0],
                          split.col_mask(cs))
        stage = ro.bit_length() - 1
        held = ro - (1 << stage)
        src = weight_own(my_col) if (cs, held) == (0, 0) else weight_slot(cs, held)
        return remote(src, weight_slot(cs, held), w_send.at[cs, ro], w_recv.at[cs, ro],
                      [split.row[stage]])

    def row_copy(own, out, send, recv, co, k):
        stage = co.bit_length() - 1
        held = co - (1 << stage)
        src = own.at[pl.ds(k * piece, piece)] if held == 0 else row_slot(out, held, k)
        return remote(src, row_slot(out, held, k), send.at[co, k], recv.at[co, k],
                      [split.col[stage]])

    def start_weight(cs, ro):
        copy = weight_copy(cs, ro)
        copy.start()
        sent.append(copy)

    def start_row(co, k):
        copy = row_copy(n_ref, n_out, n_send, n_recv, co, k)
        copy.start()
        sent.append(copy)
        gcopy = row_copy(g_ref, g_out, g_send, g_recv, co, k)

        @pl.when(decoder)
        def _():
            gcopy.start()

        gsent.append(gcopy)

    row_stages = len(split.row)
    col_stages = len(split.col)

    def have_weight(cs, ro):
        first = ro.bit_length()
        for stage in range(first, row_stages):
            start_weight(cs, ro + (1 << stage))

    def have_row(co, k):
        for stage in range(co.bit_length(), col_stages):
            start_row(co + (1 << stage), k)

    for cs in range(1, ncol):
        start_weight(cs, 0)
    have_weight(0, 0)

    own = [
        pltpu.make_async_copy(weight_own(my_col), weight_slot(0, 0), own_sem.at[0]),
        pltpu.make_async_copy(
            n_ref, n_out.at[pl.ds(pl.multiple_of(my_col * rows, rows), rows)], own_sem.at[1]
        ),
        pltpu.make_async_copy(
            g_ref, g_out.at[pl.ds(pl.multiple_of(my_col * rows, rows), rows)], own_sem.at[2]
        ),
    ]
    for copy in own:
        copy.start()

    for cs in range(1, ncol):
        weight_copy(cs, 0).wait_recv()
        have_weight(cs, 0)
        for stage in range(col_stages):
            if cs == 1 << stage:
                for k in range(pieces):
                    start_row(cs, k)

    weights = [(ro.bit_length() == row_stages, ro, cs) for ro in range(1, nrow) for cs in range(ncol)]
    row_steps = [(co.bit_length() == col_stages, co, k) for co in range(1, ncol) for k in range(pieces)]
    order = []
    for last in (False, True):
        some = sorted(w for w in weights if w[0] == last)
        order += [(last, (i + 1) / len(some), 0, (cs, ro)) for i, (_, ro, cs) in enumerate(some)]
        some = sorted(r for r in row_steps if r[0] == last)
        order += [(last, (i + 1) / len(some), 1, (co, k)) for i, (_, co, k) in enumerate(some)]
    order = [entry[1:] for entry in sorted(order)]
    for _, kind, block in order:
        if kind == 0:
            weight_copy(*block).wait_recv()
            have_weight(*block)
        else:
            row_copy(n_ref, n_out, n_send, n_recv, *block).wait_recv()
            gcopy = row_copy(g_ref, g_out, g_send, g_recv, *block)

            @pl.when(decoder)
            def _():
                gcopy.wait_recv()

            have_row(*block)

    for copy in own:
        copy.wait()
    for copy in sent:
        copy.wait_send()
    for copy in gsent:
        @pl.when(decoder)
        def _():
            copy.wait_send()


def gather(split, weights, normed, grads):
    ncol, wide = split.ncol, weights.shape[1] // split.ncol
    rows, width = normed.shape
    pieces = 2
    hbm = pl.BlockSpec(memory_space=pl.ANY)
    dma = pltpu.SemaphoreType.DMA
    return pl.pallas_call(
        functools.partial(gather_kernel, split, pieces),
        out_shape=(
            jax.ShapeDtypeStruct((width, wide), weights.dtype),
            jax.ShapeDtypeStruct((ncol * rows, width), normed.dtype),
            jax.ShapeDtypeStruct((ncol * rows, width), grads.dtype),
        ),
        in_specs=[hbm] * 3,
        out_specs=(hbm,) * 3,
        scratch_shapes=[
            dma((ncol, split.nrow)), dma((ncol, split.nrow)),
            dma((ncol, pieces)), dma((ncol, pieces)),
            dma((ncol, pieces)), dma((ncol, pieces)),
            dma((3,)),
        ],
        compiler_params=pltpu.CompilerParams(collective_id=0, has_side_effects=True),
        name="gather",
    )(weights, normed, grads)


def scatter_kernel(split, p_ref, o_ref, land, held, send, recv, out_send, out_recv, own_sem):
    me = lax.axis_index("dp")
    ncol = split.ncol
    depth = o_ref.shape[1]
    stages = list(reversed(range(len(split.row))))
    my_col = split.col_index(me)
    strip = 64

    def slot(co, ro):
        block = flipped(flipped(me, split.col_mask(co)), split.row_mask(ro))
        return pl.multiple_of(block * depth, depth)

    def copy_of(co, ro):
        stage = ro.bit_length() - 1
        kept = ro - (1 << stage)
        first = stage == stages[0]
        src = p_ref.at[pl.ds(slot(co, ro), depth)] if first else held.at[co, ro]
        return pltpu.make_async_remote_copy(
            src_ref=src, dst_ref=land.at[co, ro], send_sem=send.at[co, ro], recv_sem=recv.at[co, ro],
            device_id={"dp": flipped(me, [split.row[stage]])}, device_id_type=MESH,
        )

    def out_copy(co):
        src = held.at[co, 0]
        return pltpu.make_async_remote_copy(
            src_ref=src, dst_ref=o_ref.at[my_col], send_sem=out_send.at[co], recv_sem=out_recv.at[co],
            device_id={"dp": flipped(me, split.col_mask(co))}, device_id_type=MESH,
        )

    greet(me, split)
    copies = []
    top = 1 << stages[0]
    order = list(reversed(range(ncol)))
    for ro in reversed(range(top)):
        for co in order:
            copies.append(copy_of(co, top + ro))
    queue = list(copies)
    for copy in queue[:ncol]:
        copy.start()
    queue = queue[ncol:]
    for stage in stages:
        bit = 1 << stage
        for ro in reversed(range(bit)):
            for co in order:
                copy_of(co, bit + ro).wait_recv()
                base = slot(co, ro)
                first = stage == stages[0]
                if first and queue:
                    queue.pop(0).start()

                @pl.loop(0, depth // strip)
                def _(i):
                    at = pl.ds(pl.multiple_of(i * strip, strip), strip)
                    if first:
                        mine = p_ref[pl.ds(pl.multiple_of(base + i * strip, strip), strip)]
                    else:
                        mine = held[co, ro, at]
                    other = land[co, bit + ro, at]
                    held[co, ro, at] = (
                        mine.astype(jnp.float32) + other.astype(jnp.float32)
                    ).astype(jnp.bfloat16)

                if ro and ro.bit_length() == stage:
                    copy = copy_of(co, ro)
                    copy.start()
                    copies.append(copy)
                elif ro == 0 and stage == 0:
                    if co:
                        copy = out_copy(co)
                        copy.start()
                        copies.append(copy)
                    else:
                        own = pltpu.make_async_copy(held.at[0, 0], o_ref.at[my_col], own_sem)
                        own.start()
    for co in range(1, ncol):
        out_copy(co).wait_recv()
    own.wait()
    for copy in copies:
        copy.wait_send()


def scatter(split, part, depth):
    ncol, nrow = split.ncol, split.nrow
    wide = part.shape[1]
    dma = pltpu.SemaphoreType.DMA
    vmem = pl.BlockSpec(memory_space=pltpu.VMEM)
    return pl.pallas_call(
        functools.partial(scatter_kernel, split),
        out_shape=jax.ShapeDtypeStruct((ncol, depth, wide), part.dtype),
        in_specs=[vmem],
        out_specs=vmem,
        scratch_shapes=[
            pltpu.VMEM((ncol, nrow, depth, wide), part.dtype),
            pltpu.VMEM((ncol, nrow // 2, depth, wide), part.dtype),
            dma((ncol, nrow)), dma((ncol, nrow)), dma((ncol,)), dma((ncol,)), dma,
        ],
        compiler_params=pltpu.CompilerParams(
            collective_id=1, has_side_effects=True, vmem_limit_bytes=48 * 1024 * 1024
        ),
        name="scatter",
    )(part)


def shards(split, states, loss_grad, gains, w_param, w_fixed, probes):
    ncol, nrow = split.ncol, split.nrow
    is_encoder = lax.axis_index("grp") == 0
    seqs_own, length, width = states.shape[1:]
    rows_own = seqs_own * length
    depth = w_param.shape[1]
    cols_mp = w_param.shape[2]
    cols = cols_mp // ncol
    probe_count = probes.shape[2]
    rows = rows_own * ncol

    normed_own = normalize(states[0].reshape(rows_own, width), gains[0])
    grads_own = loss_grad.reshape(rows_own, width)

    units = [w_param[0], *(probes[0, :, p] for p in range(probe_count)), w_fixed[0]]
    wcat = jnp.concatenate(
        [unit[:, c * cols : (c + 1) * cols] for c in range(ncol) for unit in units], axis=1
    )
    w_all, normed, grads = gather(split, wcat, normed_own, grads_own)
    source = jnp.where(is_encoder, normed, grads)

    wide = (1 + probe_count) * cols
    first = jnp.dot(normed, w_all[:, :wide], preferred_element_type=jnp.float32).astype(jnp.bfloat16)
    second = jnp.dot(source, w_all[:, wide:], preferred_element_type=jnp.float32).astype(jnp.bfloat16)

    half = rows // 2
    grp = lax.axis_index("grp")

    def halves(x):
        keep = lax.dynamic_slice_in_dim(x, grp * half, half, 0)
        return keep, swapped(lax.dynamic_slice_in_dim(x, (1 - grp) * half, half, 0))

    keep, other = halves(first)
    keep_last, other_last = halves(second)
    weight = float(rows_own * ncol * nrow) ** (-0.5)
    own, theirs = attention(keep, keep_last, other, other_last, length, probe_count, weight)
    back = swapped(theirs)
    chosen = jnp.concatenate(
        [jnp.where(is_encoder, own, back), jnp.where(is_encoder, back, own)], axis=0
    )
    part = lax.dot_general(
        normed, chosen, (((0,), (0,)), ((), ())), preferred_element_type=jnp.float32
    ).astype(jnp.bfloat16)
    out = scatter(split, part, depth)
    out = jnp.transpose(out.reshape(ncol, depth, probe_count, cols), (1, 2, 0, 3))
    return out.reshape(1, depth, probe_count, cols_mp)


def solution(mesh):
    dp, mp = (mesh.shape[name] for name in ("dp", "mp"))
    in_specs = (
        P("grp", "dp", None, None),
        P("dp", None, None),
        P("grp", None),
        P("grp", "dp", "mp"),
        P("grp", "dp", "mp"),
        P("grp", "dp", None, "mp"),
    )
    out_specs = P("grp", "dp", None, "mp")

    def run(states, loss_grad, gains, w_param, w_fixed, probes):
        split = Split(dp, w_param.shape[2] // mp // HEAD)
        return jax.shard_map(
            functools.partial(shards, split),
            mesh=mesh, in_specs=in_specs, out_specs=out_specs, check_vma=False,
        )(states, loss_grad, gains, w_param, w_fixed, probes)

    return run
```
